256 devices in a mesh: pipe: 8 (over z), section: 4 (over y_hi, core), tensor: 8 (over x, y_lo).
Axes of the slice: x: 4, y: 4 (y_hi: 2, y_lo: 2; y = y_hi * 2 + y_lo), z: 8, core: 2. Of those that a mesh axis runs over, the one named last changes fastest.
Arguments:
- tokens: bfloat16 [8, 4, 2, 256, 8192], P('pipe', 'section', None, None, 'tensor'), may hold values from -51 to 51
- norm_gain: bfloat16 [4, 8192], P('section', 'tensor'), may hold values from 0.25 to 1.75
- held_kv: bfloat16 [4, 8192, 2048], P('section', 'tensor', 'pipe'), may hold values from -0.0625 to 0.0625
- block_holder: int32 [4, 8], replicated, may hold values from 0 to 7, each once within a row
- section_layer: int32 [8, 4], replicated, may hold values from 0 to 3, each once within a row
- cotangent: bfloat16 [8, 4, 2, 256, 2048], P('pipe', 'section', None, None, 'tensor'), may hold values from -6 to 6
Outputs:
- keys_values: bfloat16 [8, 4, 2, 256, 2048], P('pipe', 'section', None, None, 'tensor')
- token_grad: bfloat16 [8, 4, 2, 256, 8192], P('pipe', 'section', None, None, 'tensor')
- kv_grads: bfloat16 [4, 8192, 2048], P('section', 'tensor', 'pipe')
The draws below stay inside these ranges and needn't reach their ends.
Inputs may be any that keep to these rules, and one draw needn't show every extreme that they name: Each row of section_layer is a permutation of the 4 window layers. Each row of block_holder is a permutation of the 8 relays.
All inputs are finite; a program needn't handle non-finite values.
Results may differ from the reference program's by a relative error of at most 0.0057.
Values may be sent and summed in bfloat16 or wider, within the bound.
No kernel may reach another device: no remote copies, remote signals or barrier semaphores. Data moves between devices by JAX's collectives and lax.ppermute only.
A program may use at most 128 MiB of HBM per device.

```python
import math
import jax
import jax.numpy as jnp
from jax import lax

D = 8192
MB = 2
TOK = 256
KVW = 2048
LAYERS = 4
N_PIPE = 8
N_SECTION = 4


def draw_tokens(key, part):
    key = jax.random.fold_in(key, 17)
    key_base, key_rows, key_cols = jax.random.split(key, 3)
    full_shape = (N_PIPE, N_SECTION, MB, TOK, D)
    base_draw = jnp.clip(jax.random.normal(key_base, full_shape, jnp.float32), -4.0, 4.0)
    row_scale = jnp.exp(jax.random.uniform(key_rows, (N_PIPE, N_SECTION, MB, TOK, 1), jnp.float32, math.log(0.3), math.log(3.0)))
    feature_ramp = jnp.arange(D, dtype=jnp.float32) / (D - 1)
    col_scale = 0.3 * jnp.exp(feature_ramp * math.log(10.0)) * jax.random.uniform(key_cols, (D,), jnp.float32, 0.7, 1.4)
    return (base_draw * row_scale * col_scale).astype(jnp.bfloat16)


def block_levels(rng, dims, cuts, low, largest):
    def one(axis_at, shards_of):
        steps = jax.random.uniform(jax.random.fold_in(jax.random.fold_in(rng, 6), axis_at), (shards_of,), jnp.float32, low / len(cuts), largest / len(cuts))
        return jnp.repeat(jnp.exp(steps), dims[axis_at] // shards_of).reshape((-1,) + (1,) * (len(dims) - axis_at - 1))

    loudness = one(*cuts[0])
    for cut in cuts[1:]:
        loudness = loudness * one(*cut)
    return loudness


def normal_values(own_key, extent, width, reach, pieces=(), kind=jnp.bfloat16):
    values = width * jax.random.normal(own_key, extent, jnp.float32)
    if pieces:
        values = values * block_levels(own_key, extent, pieces, -0.22, 0.18)
    return jnp.clip(values, -reach, reach).astype(kind)


def setup_inputs(seed: int = 0) -> dict:
    key_of = jax.random.split(jax.random.key(seed), 7)
    tokens = draw_tokens(jax.random.fold_in(key_of[6], 71), 0)
    norm_gain = jnp.clip(1.0 + 0.15 * jax.random.normal(key_of[1], (LAYERS, D), jnp.float32), 0.25, 1.75).astype(jnp.bfloat16)
    held_kv = normal_values(key_of[2], (LAYERS, D, KVW), D ** -0.5, 0.0625, ((0, 4), (1, 8), (2, 8)))
    block_holder = jax.vmap(lambda own: jax.random.permutation(own, N_PIPE))(jax.random.split(key_of[3], LAYERS)).reshape((LAYERS, N_PIPE)).astype(jnp.int32)
    section_layer = jax.vmap(lambda own: jax.random.permutation(own, N_SECTION))(jax.random.split(key_of[4], N_PIPE)).reshape((N_PIPE, N_SECTION)).astype(jnp.int32)
    cotangent = normal_values(key_of[5], (N_PIPE, N_SECTION, MB, TOK, KVW), 1.0, 6.0, ((0, 8), (1, 4), (4, 8)))
    return {"tokens": tokens, "norm_gain": norm_gain, "held_kv": held_kv, "block_holder": block_holder, "section_layer": section_layer, "cotangent": cotangent}


EPSILON = 1e-05

def invert_slots(holder_row):
    slot_count = holder_row.shape[0]
    slot_ids = jnp.arange(slot_count, dtype=jnp.int32)
    slot_match = holder_row[None, :] == slot_ids[:, None]
    return lax.optimization_barrier(jnp.sum(jnp.where(slot_match, slot_ids[None, :], 0), axis=1)).astype(jnp.int32)

def unpack_layer(held_kv, block_holder, layer_index):
    stored = held_kv[layer_index].reshape(D, N_PIPE, KVW // N_PIPE)
    return jnp.take(stored, block_holder[layer_index], axis=1).reshape(D, KVW)

def reference(tokens, norm_gain, held_kv, block_holder, section_layer, cotangent):
    row_count = MB * TOK

    def one_device(grads, item):
        pipe_index = item // N_SECTION
        section_index = item % N_SECTION
        layer_index = section_layer[pipe_index, section_index]
        weight = unpack_layer(held_kv, block_holder, layer_index)
        inputs = tokens[pipe_index, section_index].reshape(row_count, D).astype(jnp.float32)
        squares = lax.optimization_barrier(jnp.mean(inputs * inputs, axis=1))
        scale_rows = lax.rsqrt(squares + EPSILON)
        layer_gain = norm_gain[layer_index].astype(jnp.float32)
        normed = (inputs * scale_rows[:, None] * layer_gain).astype(jnp.bfloat16)
        keys_values = jnp.dot(normed, weight, preferred_element_type=jnp.float32).astype(jnp.bfloat16)
        upstream = cotangent[pipe_index, section_index].reshape(row_count, KVW)
        normed_grad = jnp.dot(upstream, weight.T, preferred_element_type=jnp.float32)
        rounded = lax.optimization_barrier(jnp.dot(normed.T, upstream, preferred_element_type=jnp.float32).astype(jnp.bfloat16))
        grads = grads.at[layer_index].add(rounded.astype(jnp.float32))
        row_inner = lax.optimization_barrier(jnp.sum(layer_gain * normed_grad * inputs, axis=1))
        token_grad = (scale_rows[:, None] * layer_gain * normed_grad - inputs * (scale_rows ** 3 * row_inner / D)[:, None]).astype(jnp.bfloat16)
        return (grads, (keys_values, token_grad))
    start = jnp.zeros((N_SECTION, D, KVW), jnp.float32)
    grads, (all_kv, all_grad) = lax.scan(one_device, start, jnp.arange(N_PIPE * N_SECTION, dtype=jnp.int32))

    def pack_layer(layer_index):
        blocks = grads[layer_index].reshape(D, N_PIPE, KVW // N_PIPE)
        return jnp.take(blocks, invert_slots(block_holder[layer_index]), axis=1).reshape(D, KVW)
    packed = lax.map(pack_layer, jnp.arange(N_SECTION, dtype=jnp.int32))
    keys_values = all_kv.reshape(N_PIPE, N_SECTION, MB, TOK, KVW)
    token_grad = all_grad.reshape(N_PIPE, N_SECTION, MB, TOK, D)
    return (keys_values, token_grad, packed.astype(jnp.bfloat16))
```

```python
import functools

import jax
import jax.numpy as jnp
from jax import lax
from jax.experimental import pallas as pl
from jax.experimental.pallas import tpu as pltpu
from jax.sharding import PartitionSpec as P

EPSILON = 1e-05
EXTRA = 16
F32 = jnp.float32
BF16 = jnp.bfloat16


def invert(row):
    ids = jnp.arange(row.shape[0], dtype=jnp.int32)
    return jnp.sum(jnp.where(row[None, :] == ids[:, None], ids[None, :], 0), axis=1)


def swap(x, axis, bits):
    size = lax.axis_size(axis)
    return lax.ppermute(x, axis, [(i, i ^ bits) for i in range(size)])


def shift(x, axis, step):
    size = lax.axis_size(axis)
    return lax.ppermute(x, axis, [(i, (i + step) % size) for i in range(size)])


def y_swap(x, hi, lo):
    sections, tensors = lax.axis_size("section"), lax.axis_size("tensor")
    pairs = [
        (s * tensors + t, (s ^ (2 * hi)) * tensors + (t ^ lo))
        for s in range(sections)
        for t in range(tensors)
    ]
    return lax.ppermute(x, ("section", "tensor"), pairs)


def split_rows(row_values):
    tiled = row_values.reshape(-1, 256)
    high = lax.reduce_precision(tiled, 8, 7)
    both = jnp.concatenate([high, tiled - high], axis=0)
    return jnp.pad(both, ((0, EXTRA - both.shape[0]), (0, 0))).astype(BF16)


def exchange(x, mine, sibling):
    across = swap(x, "section", 2)
    outgoing = jnp.where(sibling == 3, across, x)
    other = swap(outgoing, "section", 1)
    return jnp.where(mine == 0, x, jnp.where(mine == 2, across, other))


def dw_kernel(slot_ref, normed_ref, g0, g1, g2, g3, out_ref):
    rows, feats = normed_ref.shape
    pieces = (g0, g1, g2, g3)
    for f in range(0, feats, 256):
        turned = normed_ref[:, f : f + 256].T
        for q in range(8):
            grads = jnp.dot(
                turned, pieces[q // 2][q % 2, :rows, :], preferred_element_type=F32
            )
            out_ref[slot_ref[q], f : f + 256, :] = grads.astype(BF16)


def main_kernel(slot_ref, place_ref, normed_ref, x_ref, r_ref, gain_ref, g0, g1, g2, g3, *rest):
    w_refs, (y_ref, a_ref, g_slots, total) = rest[:16], rest[16:]
    rows, feats = normed_ref.shape
    half = feats // 2
    pieces = (g0, g1, g2, g3)
    for q in range(8):
        g_slots[slot_ref[q]] = pieces[q // 2][q % 2, :rows, :]
    for d in range(8):
        upper, lower = w_refs[2 * d], w_refs[2 * d + 1]
        y = jnp.dot(normed_ref[:, :half], upper[...], preferred_element_type=F32)
        y += jnp.dot(normed_ref[:, half:], lower[...], preferred_element_type=F32)
        y_ref[place_ref[d], :rows, :] = y.astype(BF16)
        for h, w_ref in ((0, upper), (half, lower)):
            term = lax.dot_general(
                g_slots[d], w_ref[...], (((1,), (1,)), ((), ())), preferred_element_type=F32
            )
            if d == 0:
                total[:, h : h + half] = term
            else:
                total[:, h : h + half] += term
    scaled = total[...] * gain_ref[...].astype(F32)
    inner = jnp.sum(scaled * x_ref[...].astype(F32), axis=1, keepdims=True)
    a_ref[...] = (scaled * r_ref[...]).astype(BF16)
    line = jnp.broadcast_to(inner, (rows, 128)).T[0:1, :]
    high = line.astype(BF16).astype(F32)
    low = line - high
    row = lax.broadcasted_iota(jnp.int32, (EXTRA, 256), 0)
    tile = jnp.zeros((EXTRA, 256), F32)
    for i, part in enumerate((high[:, :256], high[:, 256:], low[:, :256], low[:, 256:])):
        tile = jnp.where(row == i, jnp.broadcast_to(part, (EXTRA, 256)), tile)
    for q in range(8):
        y_ref[q, rows:, :] = tile.astype(BF16)


VMEM = pl.BlockSpec(memory_space=pltpu.VMEM)
SMEM = pl.BlockSpec(memory_space=pltpu.SMEM)


def per_device(tokens, norm_gain, held_kv, block_holder, section_layer, cotangent):
    pipe = lax.axis_index("pipe")
    section = lax.axis_index("section")
    tensor = lax.axis_index("tensor")
    pipes = lax.axis_size("pipe")
    tensors = lax.axis_size("tensor")
    micro, tok, feats = tokens.shape[2:]
    rows = micro * tok
    model = feats * tensors
    held = held_kv[0]
    half = feats // 2
    cols = held.shape[1]

    layers = section_layer[pipe]
    sources = invert(layers)
    take_in = (sources[section] ^ section, sources[section ^ 1] ^ section ^ 1)
    take_out = (layers[section] ^ section, layers[section ^ 1] ^ section ^ 1)

    upper, lower = [None] * pipes, [None] * pipes
    upper[0], lower[0] = held[:half], held[half:]
    for d in range(1, 5):
        upper[d] = shift(upper[d - 1], "pipe", -1)
        if d < 4:
            lower[d] = shift(lower[d - 1], "pipe", -1)
        e = pipes - d
        lower[e] = shift(lower[(e + 1) % pipes], "pipe", 1)
        if d < 4:
            upper[e] = shift(upper[(e + 1) % pipes], "pipe", 1)

    x_own = tokens.reshape(rows, feats)
    squares = jnp.sum(jnp.square(x_own.astype(F32)), axis=1)
    piece = jnp.concatenate([cotangent.reshape(rows, -1), split_rows(squares)], axis=0)
    here = jnp.stack([piece, y_swap(piece, 0, 1)])
    there = jnp.stack([y_swap(piece, 1, 0), y_swap(piece, 1, 1)])
    other = swap(jnp.where(take_in[1] >= 2, there, here), "section", 1)
    g_near = jnp.where(take_in[0] == 0, here, jnp.where(take_in[0] == 2, there, other))
    g_parts = [g_near] + [swap(g_near, "tensor", 2 * i) for i in range(1, 4)]

    x = exchange(x_own, *take_in)

    lines = sum(jnp.sum(g[:, rows : rows + 4, :].astype(F32), axis=0) for g in g_parts)
    mean = (lines[:2] + lines[2:]).reshape(rows, 1) / model
    r = lax.rsqrt(mean + EPSILON)
    gain = norm_gain.astype(F32)
    normed = (x.astype(F32) * r * gain).astype(BF16)

    holders = block_holder[section]
    ids = jnp.arange(tensors, dtype=jnp.int32)
    slots = jnp.take(holders, ids ^ tensor)
    slots = lax.rem(slots - pipe + pipes, pipes)
    places = invert(slots)

    dw = pl.pallas_call(
        dw_kernel,
        out_shape=jax.ShapeDtypeStruct((pipes, feats, cols), BF16),
        in_specs=[SMEM] + [VMEM] * 5,
        out_specs=VMEM,
        compiler_params=pltpu.CompilerParams(vmem_limit_bytes=24 * 2**20),
        cost_estimate=pl.CostEstimate(
            flops=2 * rows * feats * cols * pipes, bytes_accessed=7 * 2**20, transcendentals=0
        ),
        name="weight_grads",
    )(slots, normed, *g_parts)

    weights = [part for d in range(pipes) for part in (upper[d], lower[d])]
    y, a = pl.pallas_call(
        main_kernel,
        out_shape=(
            jax.ShapeDtypeStruct((tensors, rows + EXTRA, cols), BF16),
            jax.ShapeDtypeStruct((rows, feats), BF16),
        ),
        in_specs=[SMEM, SMEM] + [VMEM] * (8 + len(weights)),
        out_specs=(VMEM, VMEM),
        scratch_shapes=[
            pltpu.VMEM((pipes, rows, cols), BF16),
            pltpu.VMEM((rows, feats), F32),
        ],
        compiler_params=pltpu.CompilerParams(vmem_limit_bytes=40 * 2**20),
        cost_estimate=pl.CostEstimate(
            flops=4 * rows * feats * cols * pipes, bytes_accessed=10 * 2**20, transcendentals=0
        ),
        name="keys_values_and_token_grads",
    )(slots, places, normed, x, r, norm_gain, *g_parts, *weights)

    def add(arrived, own):
        return (arrived.astype(F32) + own.astype(F32)).astype(BF16)

    def ring(part, first, last, step):
        running = part[first]
        for d in range(first - step, last, -step):
            running = add(shift(running, "pipe", step), part[d])
        return shift(running, "pipe", step)

    dw_up = dw[:, :half]
    dw_lo = dw[:, half:]
    up_plus, lo_plus = ring(dw_up, 4, 0, 1), ring(dw_lo, 3, 0, 1)
    up_minus, lo_minus = ring(dw_up, 5, 8, -1), ring(dw_lo, 4, 8, -1)
    final_up = dw_up[0].astype(F32) + up_plus.astype(F32) + up_minus.astype(F32)
    final_lo = dw_lo[0].astype(F32) + lo_plus.astype(F32) + lo_minus.astype(F32)
    kv_grads = jnp.concatenate([final_up, final_lo], axis=0).astype(BF16)[None]

    total = y[0].astype(F32)
    for q in range(1, tensors):
        total += swap(y[q], "tensor", q).astype(F32)
    inner = total[rows : rows + 2] + total[rows + 2 : rows + 4]
    coef = (r * r * r).reshape(-1, 256) * inner / model
    packed = jnp.concatenate([total[:rows].astype(BF16), split_rows(coef)], axis=0)
    packed = exchange(packed, *take_out)
    keys_values = packed[:rows].reshape(cotangent.shape)
    lines = packed[rows : rows + 4].astype(F32)
    coef = (lines[:2] + lines[2:]).reshape(rows, 1)

    a = exchange(a, *take_out)
    token_grad = (a.astype(F32) - x_own.astype(F32) * coef).astype(BF16)
    return (keys_values, token_grad.reshape(tokens.shape), kv_grads)


def solution(mesh):
    placed = (
        P("pipe", "section", None, None, "tensor"),
        P("section", "tensor"),
        P("section", "tensor", "pipe"),
        P(),
        P(),
        P("pipe", "section", None, None, "tensor"),
    )
    return jax.shard_map(
        per_device,
        mesh=mesh,
        in_specs=placed,
        out_specs=(
            P("pipe", "section", None, None, "tensor"),
            P("pipe", "section", None, None, "tensor"),
            P("section", "tensor", "pipe"),
        ),
        check_vma=False,
    )
```

```python
import functools

import jax
import jax.numpy as jnp
from jax import lax
from jax.experimental import pallas as pl
from jax.experimental.pallas import tpu as pltpu
from jax.sharding import PartitionSpec as P

EPSILON = 1e-05
EXTRA = 16
F32 = jnp.float32
BF16 = jnp.bfloat16


def invert(row):
    ids = jnp.arange(row.shape[0], dtype=jnp.int32)
    return jnp.sum(jnp.where(row[None, :] == ids[:, None], ids[None, :], 0), axis=1)


def swap(x, axis, bits):
    size = lax.axis_size(axis)
    return lax.ppermute(x, axis, [(i, i ^ bits) for i in range(size)])


def shift(x, axis, step):
    size = lax.axis_size(axis)
    return lax.ppermute(x, axis, [(i, (i + step) % size) for i in range(size)])


def after(x, *others):
    return lax.optimization_barrier((x, *others))[0]


def choose(flag, x, y):
    flag = flag.reshape((1,) * x.ndim)
    return jnp.where(jnp.broadcast_to(flag, x.shape) != 0, x, y)


def split_rows(row_values):
    tiled = row_values.reshape(-1, 256)
    high = lax.reduce_precision(tiled, 8, 7)
    both = jnp.concatenate([high, tiled - high], axis=0)
    return jnp.pad(both, ((0, EXTRA - both.shape[0]), (0, 0))).astype(BF16)


def y_pairs(hi, lo):
    return [
        (s * 8 + t, (s ^ (2 * hi)) * 8 + (t ^ lo)) for s in range(4) for t in range(8)
    ]


def y_swap(x, hi, lo):
    return lax.ppermute(x, ("section", "tensor"), y_pairs(hi, lo))


def split_rows(row_values):
    tiled = row_values.reshape(-1, 256)
    high = lax.reduce_precision(tiled, 8, 7)
    both = jnp.concatenate([high, tiled - high], axis=0)
    return jnp.pad(both, ((0, EXTRA - both.shape[0]), (0, 0))).astype(BF16)


def y_pairs(hi, lo):
    return [
        (s * 8 + t, (s ^ (2 * hi)) * 8 + (t ^ lo)) for s in range(4) for t in range(8)
    ]


def y_swap(x, hi, lo):
    return lax.ppermute(x, ("section", "tensor"), y_pairs(hi, lo))


def pick(parts, index):
    out = parts[0]
    for i in range(1, len(parts)):
        out = jnp.where(index == i, parts[i], out)
    return out


def dw_kernel(slot_ref, normed_ref, g0, g1, g2a, g2b, g3, *outs):
    rows, feats = normed_ref.shape
    half = feats // 2
    pieces = (g0.at[0], g0.at[1], g1.at[0], g1.at[1], g2a, g2b, g3.at[0], g3.at[1])
    g_ref = outs[9]
    for q in range(8):
        g_ref[slot_ref[q]] = pieces[q][:rows, :]
    for f in range(0, feats, 256):
        turned = normed_ref[:, f : f + 256].T
        for d in range(8):
            grads = jnp.dot(turned, g_ref[d], preferred_element_type=F32).astype(BF16)
            if d != 4:
                outs[d][f : f + 256, :] = grads
            elif f < half:
                outs[4][f : f + 256, :] = grads
            else:
                outs[8][f - half : f - half + 256, :] = grads


def y_kernel(model, place_ref, normed_ref, r_ref, g_ref, *rest):
    w_refs, y_ref = rest[:9], rest[9]
    rows, feats = normed_ref.shape
    half = feats // 2
    inner = None
    for d in range(8):
        if d == 4:
            y = jnp.dot(normed_ref[:, :half], w_refs[4][...], preferred_element_type=F32)
            y += jnp.dot(normed_ref[:, half:], w_refs[8][...], preferred_element_type=F32)
        else:
            y = jnp.dot(normed_ref[...], w_refs[d][...], preferred_element_type=F32)
        y_ref[place_ref[d], :rows, :] = y.astype(BF16)
        term = y * g_ref[d].astype(F32)
        inner = term if inner is None else inner + term
    inner = jnp.sum(inner, axis=1, keepdims=True) * r_ref[...] * r_ref[...] * (1.0 / model)
    line = jnp.broadcast_to(inner, (rows, 128)).T[0:1, :]
    high = line.astype(BF16).astype(F32)
    low = line - high
    row = lax.broadcasted_iota(jnp.int32, (EXTRA, 256), 0)
    tile = jnp.zeros((EXTRA, 256), F32)
    for i, part in enumerate((high[:, :256], high[:, 256:], low[:, :256], low[:, 256:])):
        tile = jnp.where(row == i, jnp.broadcast_to(part, (EXTRA, 256)), tile)
    for b in range(8):
        y_ref[b, rows:, :] = tile.astype(BF16)


def a_kernel(r_ref, gain_ref, g_ref, *rest):
    w_refs, (a_ref, total) = rest[:9], rest[9:]
    rows, feats = total.shape
    half = feats // 2
    for d in range(8):
        g = g_ref[d]
        for h in range(2):
            if d == 4:
                w = w_refs[4 + 4 * h][...]
            else:
                w = w_refs[d][h * half : (h + 1) * half, :]
            term = lax.dot_general(
                g, w, (((1,), (1,)), ((), ())), preferred_element_type=F32
            )
            if d == 0:
                total[:, h * half : (h + 1) * half] = term
            else:
                total[:, h * half : (h + 1) * half] += term
    a_ref[...] = (total[...] * gain_ref[...].astype(F32) * r_ref[...]).astype(BF16)


def add_kernel(arrived_ref, own_ref, out_ref):
    out_ref[...] = (arrived_ref[...].astype(F32) + own_ref[...].astype(F32)).astype(BF16)


def join_kernel(cut, arrived_ref, own_ref, out_ref):
    half = arrived_ref.shape[0]
    own = own_ref[cut : cut + half, :].astype(F32)
    out_ref[cut : cut + half, :] = (arrived_ref[...].astype(F32) + own).astype(BF16)
    out_ref[half - cut : 2 * half - cut, :] = own_ref[half - cut : 2 * half - cut, :]


def last_kernel(plus_ref, minus_ref, own_ref, out_ref):
    total = own_ref[...].astype(F32) + plus_ref[...].astype(F32) + minus_ref[...].astype(F32)
    out_ref[...] = total.astype(BF16)


VMEM = pl.BlockSpec(memory_space=pltpu.VMEM)
SMEM = pl.BlockSpec(memory_space=pltpu.SMEM)
ANY = pl.BlockSpec(memory_space=pl.ANY)


def kernel_call(body, name, out_shape, operands, flops, nbytes, scratch=(), index=1):
    return pl.pallas_call(
        body,
        out_shape=out_shape,
        in_specs=[SMEM] * index + [VMEM] * (len(operands) - index),
        out_specs=[VMEM] * len(out_shape),
        scratch_shapes=list(scratch),
        compiler_params=pltpu.CompilerParams(vmem_limit_bytes=16 * 2**20),
        cost_estimate=pl.CostEstimate(flops=flops, bytes_accessed=nbytes, transcendentals=0),
        name=name,
    )(*operands)


def combine(body, name, own, *arrived):
    return pl.pallas_call(
        body,
        out_shape=jax.ShapeDtypeStruct(own.shape, BF16),
        in_specs=[VMEM] * (1 + len(arrived)),
        out_specs=VMEM,
        compiler_params=pltpu.CompilerParams(vmem_limit_bytes=6 * 2**20),
        cost_estimate=pl.CostEstimate(
            flops=own.size, bytes_accessed=6 * own.size, transcendentals=0
        ),
        name=name,
    )(*arrived, own)


def per_device(tokens, norm_gain, held_kv, block_holder, section_layer, cotangent):
    pipe = lax.axis_index("pipe")
    section = lax.axis_index("section")
    pipes = lax.axis_size("pipe")
    tensors = lax.axis_size("tensor")
    micro, tok, feats = tokens.shape[2:]
    rows = micro * tok
    model = feats * tensors
    held = held_kv[0]
    half = feats // 2
    cols = held.shape[1]

    def one(values, index):
        here = jnp.arange(values.shape[0], dtype=jnp.int32) == index
        return jnp.sum(jnp.where(here, values, 0)).reshape(1, 1)

    of_relay = jnp.arange(pipes, dtype=jnp.int32)[:, None] == pipe
    layers = jnp.sum(jnp.where(of_relay, section_layer, 0), axis=0)
    sections = invert(layers)
    every = jnp.arange(layers.shape[0], dtype=jnp.int32)
    near_sources = jnp.where((sections >> 1) == (every >> 1), 1, 0)
    core_sources = jnp.where((sections & 1) == (every & 1), 1, 0)
    near_workers = jnp.where((layers >> 1) == (every >> 1), 1, 0)
    core_workers = jnp.where((layers & 1) == (every & 1), 1, 0)
    source_near, source_core = one(near_sources, section), one(core_sources, section)
    worker_near, worker_core = one(near_workers, section), one(core_workers, section)
    far_source_core = one(core_sources, section ^ 2)
    sibling_worker_near = one(near_workers, section ^ 1)
    tensor = lax.axis_index("tensor")
    even = (1 - (tensor & 1)).reshape(1, 1)
    ids = jnp.arange(tensors, dtype=jnp.int32) ^ (tensor & ~1)
    of_layer = jnp.arange(layers.shape[0], dtype=jnp.int32)[:, None] == section
    holder_row = jnp.sum(jnp.where(of_layer, block_holder, 0), axis=0)
    holders = jnp.sum(
        jnp.where(ids[:, None] == jnp.arange(tensors)[None, :], holder_row[None, :], 0), axis=1
    )
    slots = (holders - pipe) & (pipes - 1)
    places = invert(slots)
    flags = (
        source_near,
        worker_near,
        source_core,
        worker_core,
        far_source_core,
        sibling_worker_near,
        even,
        slots,
        places,
    )

    top = rows // 2
    x_own = tokens.reshape(rows, feats)
    squares = jnp.sum(jnp.square(x_own.astype(F32)), axis=1)
    piece = jnp.concatenate([cotangent.reshape(rows, -1), split_rows(squares)], axis=0)
    up1, down1 = shift(held, "pipe", -1), shift(held, "pipe", 1)
    piece_other, x_other = swap(piece, "section", 1), swap(x_own, "section", 1)
    piece_other, x_other, flags = lax.optimization_barrier((piece_other, x_other, flags))
    (
        source_near,
        worker_near,
        source_core,
        worker_core,
        far_source_core,
        sibling_worker_near,
        even,
        slots,
        places,
    ) = flags
    piece_here = choose(source_core, piece, piece_other)
    piece_there = choose(far_source_core, piece, piece_other)
    flip_lo = y_swap(piece_here, 0, 1)
    flip_hi = y_swap(piece_there, 1, 0)
    flip_both = y_swap(piece_there, 1, 1)
    up1, down1, flip_lo, flip_hi, flip_both, x_other = lax.optimization_barrier(
        (up1, down1, flip_lo, flip_hi, flip_both, x_other)
    )

    up2, down2 = shift(up1, "pipe", -1), shift(down1, "pipe", 1)
    g_own = choose(source_near, piece_here, flip_hi)
    g_flip = choose(source_near, flip_lo, flip_both)
    pair = jnp.stack([choose(even, g_own, g_flip), choose(even, g_flip, g_own)])
    g1, g3 = swap(pair, "tensor", 2), swap(pair, "tensor", 6)
    x_there = choose(far_source_core, x_own, x_other)
    x_far0 = swap(x_there[:top], "section", 2)
    up2, down2, g1, g3, pair, x_far0, x_there = lax.optimization_barrier(
        (up2, down2, g1, g3, pair, x_far0, x_there)
    )

    up3, down3 = shift(up2, "pipe", -1), shift(down2, "pipe", 1)
    g2a, g2b = swap(g3[0], "tensor", 2), swap(g1[1], "tensor", 6)
    x_far1 = swap(x_there[top:], "section", 2)
    up3, down3, g1, g3, g2a, g2b, pair, x_far0, x_far1 = lax.optimization_barrier(
        (up3, down3, g1, g3, g2a, g2b, pair, x_far0, x_far1)
    )

    up4, down4 = shift(up3[:half], "pipe", -1), shift(down3[half:], "pipe", 1)
    x_near = choose(source_core, x_own, x_other)
    x = choose(source_near, x_near, jnp.concatenate([x_far0, x_far1], axis=0))
    g = (pair, g1, g2a, g2b, g3)
    lines = sum(
        jnp.sum(part.reshape(-1, rows + EXTRA, cols)[:, rows : rows + 4].astype(F32), axis=0)
        for part in g
    )
    mean = (lines[:2] + lines[2:]).reshape(rows, 1) / model
    r = lax.rsqrt(mean + EPSILON)
    normed = (x.astype(F32) * r * norm_gain.astype(F32)).astype(BF16)

    flops = 2 * rows * feats * cols * pipes
    whole = jax.ShapeDtypeStruct((feats, cols), BF16)
    part = jax.ShapeDtypeStruct((half, cols), BF16)
    *dw, g = kernel_call(
        dw_kernel,
        "weight_grads",
        (*[whole] * 4, part, *[whole] * 3, part, jax.ShapeDtypeStruct((pipes, rows, cols), BF16)),
        (slots, normed, *g),
        flops,
        9 * 2**20,
    )

    plus, minus = shift(dw[4], "pipe", 1), shift(dw[8], "pipe", -1)

    weights = (held, up1, up2, up3, up4, down3, down2, down1, down4)
    (y,) = kernel_call(
        functools.partial(y_kernel, model),
        "keys_values",
        (jax.ShapeDtypeStruct((tensors, rows + EXTRA, cols), BF16),),
        (places, normed, r, g, *weights),
        flops,
        9 * 2**20,
    )
    (a,) = kernel_call(
        a_kernel,
        "token_grads",
        (jax.ShapeDtypeStruct((rows, feats), BF16),),
        (r, norm_gain, after(g, y), *weights),
        flops,
        7 * 2**20,
        [pltpu.VMEM((rows, feats), F32)],
        index=0,
    )

    plus, minus, y, a = lax.optimization_barrier((plus, minus, y, a))

    def unpack(z):
        lines = z[rows : rows + 4].astype(F32)
        return lines[:2] + lines[2:]

    def total_of(parts):
        total = sum(part.astype(F32) for part in parts)
        return total[:rows].astype(BF16), unpack(total)

    def pack(total):
        return jnp.concatenate([total[0], split_rows(total[1])], axis=0)

    plus = combine(functools.partial(join_kernel, 0), "join", dw[3], plus)
    minus = combine(functools.partial(join_kernel, half), "join", dw[5], minus)
    plus, minus = shift(plus, "pipe", 1), shift(minus, "pipe", -1)
    to3, to1 = swap(y[4], "tensor", 2), swap(y[5], "tensor", 6)
    a0, a1 = a[:top], a[top:]
    a_far0 = swap(a0, "section", 2)
    plus, minus, to3, to1, a_far0, a1, y = lax.optimization_barrier(
        (plus, minus, to3, to1, a_far0, a1, y)
    )

    plus, minus = combine(add_kernel, "add", dw[2], plus), combine(add_kernel, "add", dw[6], minus)
    plus, minus = shift(plus, "pipe", 1), shift(minus, "pipe", -1)
    send1 = jnp.stack([y[2], pack(total_of([y[3], to1]))])
    send3 = jnp.stack([pack(total_of([y[6], to3])), y[7]])
    got1, got3 = swap(send1, "tensor", 2), swap(send3, "tensor", 6)
    a_far1 = swap(a1, "section", 2)
    plus, minus, got1, got3, a_far1, a0, a_far0 = lax.optimization_barrier(
        (plus, minus, got1, got3, a_far1, a0, a_far0)
    )

    plus, minus = combine(add_kernel, "add", dw[1], plus), combine(add_kernel, "add", dw[7], minus)
    plus, minus = shift(plus, "pipe", 1), shift(minus, "pipe", -1)
    parts = [y[:2], got1, got3]
    stays = pack(total_of([choose(even, p[0], p[1]) for p in parts]))
    leaves = pack(total_of([choose(even, p[1], p[0]) for p in parts]))
    flip_lo, flip_hi = y_swap(leaves, 0, 1), y_swap(stays, 1, 0)
    flip_both = y_swap(leaves, 1, 1)
    plus, minus, flip_lo, flip_hi, flip_both, a0, a1, a_far0, a_far1 = lax.optimization_barrier(
        (plus, minus, flip_lo, flip_hi, flip_both, a0, a1, a_far0, a_far1)
    )
    kv_grads = combine(last_kernel, "last", dw[0], plus, minus)[None]

    def come_back(here, across):
        other = swap(choose(sibling_worker_near, here, across), "section", 1)
        return choose(worker_core, choose(worker_near, here, across), other)

    packed = come_back(pack(total_of([stays, flip_lo])), pack(total_of([flip_hi, flip_both])))
    keys_values = packed[:rows].reshape(cotangent.shape)
    coef = unpack(packed).reshape(rows, 1)
    a = come_back(jnp.concatenate([a0, a1]), jnp.concatenate([a_far0, a_far1]))
    token_grad = (a.astype(F32) - x_own.astype(F32) * coef).astype(BF16)
    return (keys_values, token_grad.reshape(tokens.shape), kv_grads)


def solution(mesh):
    placed = (
        P("pipe", "section", None, None, "tensor"),
        P("section", "tensor"),
        P("section", "tensor", "pipe"),
        P(),
        P(),
        P("pipe", "section", None, None, "tensor"),
    )
    return jax.shard_map(
        per_device,
        mesh=mesh,
        in_specs=placed,
        out_specs=(
            P("pipe", "section", None, None, "tensor"),
            P("pipe", "section", None, None, "tensor"),
            P("section", "tensor", "pipe"),
        ),
        check_vma=False,
    )
```

```python
import functools

import jax
import jax.numpy as jnp
from jax import lax
from jax.experimental import pallas as pl
from jax.experimental.pallas import tpu as pltpu
from jax.sharding import PartitionSpec as P

EPSILON = 1e-05
EXTRA = 16
F32 = jnp.float32
BF16 = jnp.bfloat16


def invert(row):
    ids = jnp.arange(row.shape[0], dtype=jnp.int32)
    return jnp.sum(jnp.where(row[None, :] == ids[:, None], ids[None, :], 0), axis=1)


def swap(x, axis, bits):
    size = lax.axis_size(axis)
    return lax.ppermute(x, axis, [(i, i ^ bits) for i in range(size)])


def shift(x, axis, step):
    size = lax.axis_size(axis)
    return lax.ppermute(x, axis, [(i, (i + step) % size) for i in range(size)])


def after(x, *others):
    return lax.optimization_barrier((x, *others))[0]


def choose(flag, x, y):
    flag = flag.reshape((1,) * x.ndim)
    return jnp.where(jnp.broadcast_to(flag, x.shape) != 0, x, y)


def split_rows(row_values):
    tiled = row_values.reshape(-1, 256)
    high = lax.reduce_precision(tiled, 8, 7)
    both = jnp.concatenate([high, tiled - high], axis=0)
    return jnp.pad(both, ((0, EXTRA - both.shape[0]), (0, 0))).astype(BF16)


def y_pairs(hi, lo):
    return [
        (s * 8 + t, (s ^ (2 * hi)) * 8 + (t ^ lo)) for s in range(4) for t in range(8)
    ]


def y_swap(x, hi, lo):
    return lax.ppermute(x, ("section", "tensor"), y_pairs(hi, lo))


def split_rows(row_values):
    tiled = row_values.reshape(-1, 256)
    high = lax.reduce_precision(tiled, 8, 7)
    both = jnp.concatenate([high, tiled - high], axis=0)
    return jnp.pad(both, ((0, EXTRA - both.shape[0]), (0, 0))).astype(BF16)


def y_pairs(hi, lo):
    return [
        (s * 8 + t, (s ^ (2 * hi)) * 8 + (t ^ lo)) for s in range(4) for t in range(8)
    ]


def y_swap(x, hi, lo):
    return lax.ppermute(x, ("section", "tensor"), y_pairs(hi, lo))


def pick(parts, index):
    out = parts[0]
    for i in range(1, len(parts)):
        out = jnp.where(index == i, parts[i], out)
    return out


def dw_kernel(model, slot_ref, pick_ref, x_ref, other, far, gain_ref, *rest):
    g0, g1, g2a, g2b, g3, normed_ref, r_ref, g_ref, own, p1, p2, p3, p4, m1, m2, m3, m4 = rest
    rows, feats = normed_ref.shape
    top, half = rows // 2, feats // 2
    pieces = (g0.at[0], g0.at[1], g1.at[0], g1.at[1], g2a, g2b, g3.at[0], g3.at[1])
    sums = sum(piece[rows:, :].astype(F32) for piece in pieces)
    scale = lax.rsqrt((sums[:2] + sums[2:4]) / model + EPSILON)
    for h in range(2):
        here = slice(h * top, (h + 1) * top)
        r_ref[here, :] = jnp.broadcast_to(scale[h : h + 1, :], (128, top)).T
        for i, source in enumerate((x_ref, other, far)):

            @pl.when(pick_ref[0] == i)
            def _():
                scaled = source[here, :].astype(F32) * r_ref[here, 0:1]
                normed_ref[here, :] = (scaled * gain_ref[...].astype(F32)).astype(BF16)

    for q in range(8):
        g_ref[slot_ref[q]] = pieces[q][:rows, :]
    uppers = (own, p4, p3, p2, p1, m1, m2, m3)
    lowers = (own, p3, p2, p1, m1, m2, m3, m4)
    for f in range(0, feats, 256):
        turned = normed_ref[:, f : f + 256].T
        for d in range(8):
            out_ref = uppers[d] if f < half else lowers[d]
            at = f - half if out_ref is m4 else f
            grads = jnp.dot(turned, g_ref[d], preferred_element_type=F32)
            out_ref[at : at + 256, :] = grads.astype(BF16)


def weight_halves(refs):
    held, up1, up2u, up_b, up_c, down1, down2l, down_b, down_c = refs
    half = up2u.shape[0]
    up, lo = slice(0, half), slice(half, 2 * half)
    return (
        (held.at[up], held.at[lo]),
        (up1.at[up], up1.at[lo]),
        (up2u, up_b.at[lo]),
        (up_b.at[up], up_c.at[lo]),
        (up_c.at[up], down_c.at[lo]),
        (down_c.at[up], down_b.at[lo]),
        (down_b.at[up], down2l),
        (down1.at[up], down1.at[lo]),
    )


def y_kernel(model, place_ref, normed_ref, r_ref, g_ref, *rest):
    y_ref = rest[9]
    rows, feats = normed_ref.shape
    half = feats // 2
    inner = None
    for d, (upper, lower) in enumerate(weight_halves(rest[:9])):
        y = jnp.dot(normed_ref[:, :half], upper[...], preferred_element_type=F32)
        y += jnp.dot(normed_ref[:, half:], lower[...], preferred_element_type=F32)
        y_ref[place_ref[d], :rows, :] = y.astype(BF16)
        term = y * g_ref[d].astype(F32)
        inner = term if inner is None else inner + term
    inner = jnp.sum(inner, axis=1, keepdims=True) * jnp.square(r_ref[:, 0:1]) * (1.0 / model)
    line = jnp.broadcast_to(inner, (rows, 128)).T[0:1, :]
    high = line.astype(BF16).astype(F32)
    low = line - high
    row = lax.broadcasted_iota(jnp.int32, (EXTRA, 256), 0)
    tile = jnp.zeros((EXTRA, 256), F32)
    for i, part in enumerate((high[:, :256], high[:, 256:], low[:, :256], low[:, 256:])):
        tile = jnp.where(row == i, jnp.broadcast_to(part, (EXTRA, 256)), tile)
    for b in range(8):
        y_ref[b, rows:, :] = tile.astype(BF16)


def a_kernel(r_ref, gain_ref, g_ref, *rest):
    a_ref, total = rest[9:]
    rows, feats = total.shape
    half = feats // 2
    for d, halves in enumerate(weight_halves(rest[:9])):
        g = g_ref[d]
        for h in range(2):
            here = slice(h * half, (h + 1) * half)
            term = lax.dot_general(
                g, halves[h][...], (((1,), (1,)), ((), ())), preferred_element_type=F32
            )
            if d == 0:
                total[:, here] = term
            else:
                total[:, here] += term
    a_ref[...] = (total[...] * gain_ref[...].astype(F32) * r_ref[:, 0:1]).astype(BF16)


def add_kernel(arrived_ref, own_ref, out_ref):
    out_ref[...] = (arrived_ref[...].astype(F32) + own_ref[...].astype(F32)).astype(BF16)


def last_kernel(plus_ref, minus_ref, plus_u, minus_l, own_ref, out_ref):
    half = plus_u.shape[0]
    for here, x_ref, y_ref in (
        (slice(0, half), plus_u, minus_ref.at[:half]),
        (slice(half, 2 * half), minus_l, plus_ref.at[half:]),
    ):
        total = own_ref[here, :].astype(F32) + x_ref[...].astype(F32) + y_ref[...].astype(F32)
        out_ref[here, :] = total.astype(BF16)


VMEM = pl.BlockSpec(memory_space=pltpu.VMEM)
SMEM = pl.BlockSpec(memory_space=pltpu.SMEM)
ANY = pl.BlockSpec(memory_space=pl.ANY)


def kernel_call(body, name, out_shape, operands, scratch=(), index=1):
    return pl.pallas_call(
        body,
        out_shape=out_shape,
        in_specs=[SMEM] * index + [VMEM] * (len(operands) - index),
        out_specs=[VMEM] * len(out_shape),
        scratch_shapes=list(scratch),
        compiler_params=pltpu.CompilerParams(vmem_limit_bytes=24 * 2**20),
        name=name,
    )(*operands)


def combine(body, name, own, *arrived):
    return pl.pallas_call(
        body,
        out_shape=jax.ShapeDtypeStruct(own.shape, BF16),
        in_specs=[VMEM] * (1 + len(arrived)),
        out_specs=VMEM,
        compiler_params=pltpu.CompilerParams(vmem_limit_bytes=6 * 2**20),
        cost_estimate=pl.CostEstimate(
            flops=own.size, bytes_accessed=6 * own.size, transcendentals=0
        ),
        name=name,
    )(*arrived, own)


def per_device(tokens, norm_gain, held_kv, block_holder, section_layer, cotangent):
    pipe = lax.axis_index("pipe")
    section = lax.axis_index("section")
    pipes = lax.axis_size("pipe")
    tensors = lax.axis_size("tensor")
    micro, tok, feats = tokens.shape[2:]
    rows = micro * tok
    model = feats * tensors
    held = held_kv[0]
    half = feats // 2
    cols = held.shape[1]

    def one(values, index):
        here = jnp.arange(values.shape[0], dtype=jnp.int32) == index
        return jnp.sum(jnp.where(here, values, 0)).reshape(1, 1)

    of_relay = jnp.arange(pipes, dtype=jnp.int32)[:, None] == pipe
    layers = jnp.sum(jnp.where(of_relay, section_layer, 0), axis=0)
    sections = invert(layers)
    every = jnp.arange(layers.shape[0], dtype=jnp.int32)
    near_sources = jnp.where((sections >> 1) == (every >> 1), 1, 0)
    core_sources = jnp.where((sections & 1) == (every & 1), 1, 0)
    near_workers = jnp.where((layers >> 1) == (every >> 1), 1, 0)
    core_workers = jnp.where((layers & 1) == (every & 1), 1, 0)
    source_near, source_core = one(near_sources, section), one(core_sources, section)
    worker_near, worker_core = one(near_workers, section), one(core_workers, section)
    far_source_core = one(core_sources, section ^ 2)
    sibling_worker_near = one(near_workers, section ^ 1)
    tensor = lax.axis_index("tensor")
    even = (1 - (tensor & 1)).reshape(1, 1)
    ids = jnp.arange(tensors, dtype=jnp.int32) ^ (tensor & ~1)
    of_layer = jnp.arange(layers.shape[0], dtype=jnp.int32)[:, None] == section
    holder_row = jnp.sum(jnp.where(of_layer, block_holder, 0), axis=0)
    holders = jnp.sum(
        jnp.where(ids[:, None] == jnp.arange(tensors)[None, :], holder_row[None, :], 0), axis=1
    )
    slots = (holders - pipe) & (pipes - 1)
    places = invert(slots)
    pick = jnp.where(source_near != 0, jnp.where(source_core != 0, 0, 1), 2).reshape(1)
    flags = (
        worker_near,
        worker_core,
        source_near,
        source_core,
        far_source_core,
        sibling_worker_near,
        even,
        slots,
        places,
        pick,
    )

    top = rows // 2
    x_own = tokens.reshape(rows, feats)
    squares = jnp.sum(jnp.square(x_own.astype(F32)), axis=1)
    piece = jnp.concatenate([cotangent.reshape(rows, -1), split_rows(squares)], axis=0)
    held_later = after(held, piece)
    up1, down1 = shift(held_later, "pipe", -1), shift(held_later, "pipe", 1)
    piece_other, x_other = swap(piece, "section", 1), swap(x_own, "section", 1)
    piece_other, flags = lax.optimization_barrier((piece_other, flags))
    (
        worker_near,
        worker_core,
        source_near,
        source_core,
        far_source_core,
        sibling_worker_near,
        even,
        slots,
        places,
        pick,
    ) = flags
    piece_here = choose(source_core, piece, piece_other)
    piece_there = choose(far_source_core, piece, piece_other)
    flip_hi = y_swap(piece_there, 1, 0)
    up2u, down2l = after(up1[:half], piece_here, piece_there), after(down1[half:], piece_here)
    up2u, down2l = shift(up2u, "pipe", -1), shift(down2l, "pipe", 1)
    x_there = choose(far_source_core, x_own, x_other)
    g_own = after(choose(source_near, piece_here, flip_hi), x_there)
    x_far = swap(x_there, "section", 2)
    g_flip = y_swap(g_own, 0, 1)
    up2u, down2l, g_own, g_flip = lax.optimization_barrier((up2u, down2l, g_own, g_flip))

    up_b = shift(jnp.concatenate([up2u, up1[half:]], axis=0), "pipe", -1)
    down_b = shift(jnp.concatenate([down1[:half], down2l], axis=0), "pipe", 1)
    pair = jnp.stack([choose(even, g_own, g_flip), choose(even, g_flip, g_own)])
    g1, g3 = swap(pair, "tensor", 2), swap(pair, "tensor", 6)
    up_b, down_b, g1, g3, pair = lax.optimization_barrier((up_b, down_b, g1, g3, pair))

    up_c, down_c = shift(up_b, "pipe", -1), shift(down_b, "pipe", 1)
    g2a, g2b = swap(g3[0], "tensor", 2), swap(g1[1], "tensor", 6)
    up_c, down_c, g1, g3, g2a, g2b, pair, x_far = lax.optimization_barrier(
        (up_c, down_c, g1, g3, g2a, g2b, pair, x_far)
    )
    weights = (held, up1, up2u, up_b, up_c, down1, down2l, down_b, down_c)

    whole = jax.ShapeDtypeStruct((feats, cols), BF16)
    part = jax.ShapeDtypeStruct((half, cols), BF16)
    normed, r, g, own, p1, p2, p3, p4, m1, m2, m3, m4 = kernel_call(
        functools.partial(dw_kernel, model),
        "weight_grads",
        (
            jax.ShapeDtypeStruct((rows, feats), BF16),
            jax.ShapeDtypeStruct((rows, 128), F32),
            jax.ShapeDtypeStruct((pipes, rows, cols), BF16),
            *[whole] * 4,
            part,
            *[whole] * 3,
            part,
        ),
        (slots, pick, x_own, x_other, x_far, norm_gain, pair, g1, g2a, g2b, g3),
        index=2,
    )
    plus, minus = shift(p1, "pipe", 1), shift(m1, "pipe", -1)
    (a,) = kernel_call(
        a_kernel,
        "token_grads",
        (jax.ShapeDtypeStruct((rows, feats), BF16),),
        (r, norm_gain, g, *weights),
        [pltpu.VMEM((rows, feats), F32)],
        index=0,
    )
    (y,) = kernel_call(
        functools.partial(y_kernel, model),
        "keys_values",
        (jax.ShapeDtypeStruct((tensors, rows + EXTRA, cols), BF16),),
        (places, normed, r, after(g, a), *weights),
    )
    to3, to1 = swap(y[4], "tensor", 2), swap(y[5], "tensor", 6)
    a_far = swap(a, "section", 2)

    def unpack(z):
        lines = z[rows : rows + 4].astype(F32)
        return lines[:2] + lines[2:]

    def total_of(parts):
        total = sum(part.astype(F32) for part in parts)
        return total[:rows].astype(BF16), unpack(total)

    def pack(total):
        return jnp.concatenate([total[0], split_rows(total[1])], axis=0)

    plus, minus = after(plus, y), after(minus, y)
    plus, minus = combine(add_kernel, "add", p2, plus), combine(add_kernel, "add", m2, minus)
    plus, minus, to3, to1 = lax.optimization_barrier((plus, minus, to3, to1))
    plus, minus = shift(plus, "pipe", 1), shift(minus, "pipe", -1)
    send1 = jnp.stack([y[2], pack(total_of([y[3], to1]))])
    send3 = jnp.stack([pack(total_of([y[6], to3])), y[7]])
    got1, got3 = swap(send1, "tensor", 2), swap(send3, "tensor", 6)

    plus, minus = combine(add_kernel, "add", p3, plus), combine(add_kernel, "add", m3, minus)
    plus, minus, got1, got3, a_far = lax.optimization_barrier((plus, minus, got1, got3, a_far))
    plus, minus = shift(plus, "pipe", 1), shift(minus, "pipe", -1)
    parts = [y[:2], got1, got3]
    stays = pack(total_of([choose(even, p[0], p[1]) for p in parts]))
    leaves = pack(total_of([choose(even, p[1], p[0]) for p in parts]))
    flip_lo, flip_hi = y_swap(leaves, 0, 1), y_swap(stays, 1, 0)
    flip_both = y_swap(leaves, 1, 1)

    plus_u = combine(add_kernel, "add", p4, plus[:half])
    minus_l = combine(add_kernel, "add", m4, minus[half:])
    plus_u, minus_l, flip_lo, flip_hi, flip_both = lax.optimization_barrier(
        (plus_u, minus_l, flip_lo, flip_hi, flip_both)
    )
    plus_u, minus_l = shift(plus_u, "pipe", 1), shift(minus_l, "pipe", -1)

    def come_back(here, across):
        other = swap(choose(sibling_worker_near, here, across), "section", 1)
        return choose(worker_core, choose(worker_near, here, across), other)

    packed = come_back(pack(total_of([stays, flip_lo])), pack(total_of([flip_hi, flip_both])))
    keys_values = packed[:rows].reshape(cotangent.shape)
    coef = unpack(packed).reshape(rows, 1)
    a = come_back(a, a_far)
    token_grad = (a.astype(F32) - x_own.astype(F32) * coef).astype(BF16)
    kv_grads = combine(
        last_kernel, "last", own, plus, minus, after(plus_u, token_grad, packed), minus_l
    )[None]
    return (keys_values, token_grad.reshape(tokens.shape), kv_grads)


def solution(mesh):
    placed = (
        P("pipe", "section", None, None, "tensor"),
        P("section", "tensor"),
        P("section", "tensor", "pipe"),
        P(),
        P(),
        P("pipe", "section", None, None, "tensor"),
    )
    return jax.shard_map(
        per_device,
        mesh=mesh,
        in_specs=placed,
        out_specs=(
            P("pipe", "section", None, None, "tensor"),
            P("pipe", "section", None, None, "tensor"),
            P("section", "tensor", "pipe"),
        ),
        check_vma=False,
    )
```

```python
import functools

import jax
import jax.numpy as jnp
from jax import lax
from jax.experimental import pallas as pl
from jax.experimental.pallas import tpu as pltpu
from jax.sharding import PartitionSpec as P

EPSILON = 1e-05
EXTRA = 16
F32 = jnp.float32
BF16 = jnp.bfloat16


def invert(row):
    ids = jnp.arange(row.shape[0], dtype=jnp.int32)
    return jnp.sum(jnp.where(row[None, :] == ids[:, None], ids[None, :], 0), axis=1)


def swap(x, axis, bits):
    size = lax.axis_size(axis)
    return lax.ppermute(x, axis, [(i, i ^ bits) for i in range(size)])


def shift(x, axis, step):
    size = lax.axis_size(axis)
    return lax.ppermute(x, axis, [(i, (i + step) % size) for i in range(size)])


def after(x, *others):
    return lax.optimization_barrier((x, *others))[0]


def choose(flag, x, y):
    flag = flag.reshape((1,) * x.ndim)
    return jnp.where(jnp.broadcast_to(flag, x.shape) != 0, x, y)


def split_rows(row_values):
    tiled = row_values.reshape(-1, 256)
    high = lax.reduce_precision(tiled, 8, 7)
    both = jnp.concatenate([high, tiled - high], axis=0)
    return jnp.pad(both, ((0, EXTRA - both.shape[0]), (0, 0))).astype(BF16)


def y_pairs(hi, lo):
    return [
        (s * 8 + t, (s ^ (2 * hi)) * 8 + (t ^ lo)) for s in range(4) for t in range(8)
    ]


def y_swap(x, hi, lo):
    return lax.ppermute(x, ("section", "tensor"), y_pairs(hi, lo))


def split_rows(row_values):
    tiled = row_values.reshape(-1, 256)
    high = lax.reduce_precision(tiled, 8, 7)
    both = jnp.concatenate([high, tiled - high], axis=0)
    return jnp.pad(both, ((0, EXTRA - both.shape[0]), (0, 0))).astype(BF16)


def y_pairs(hi, lo):
    return [
        (s * 8 + t, (s ^ (2 * hi)) * 8 + (t ^ lo)) for s in range(4) for t in range(8)
    ]


def y_swap(x, hi, lo):
    return lax.ppermute(x, ("section", "tensor"), y_pairs(hi, lo))


def pick(parts, index):
    out = parts[0]
    for i in range(1, len(parts)):
        out = jnp.where(index == i, parts[i], out)
    return out


def dw_kernel(model, slot_ref, pick_ref, x_ref, other, far, gain_ref, *rest):
    g0, g1, g2a, g2b, g3, normed_ref, r_ref, g_ref, p1, m1 = rest
    rows, feats = normed_ref.shape
    top, half = rows // 2, feats // 2
    pieces = (g0.at[0], g0.at[1], g1.at[0], g1.at[1], g2a, g2b, g3.at[0], g3.at[1])
    sums = sum(piece[rows:, :].astype(F32) for piece in pieces)
    scale = lax.rsqrt((sums[:2] + sums[2:4]) / model + EPSILON)
    for h in range(2):
        here = slice(h * top, (h + 1) * top)
        r_ref[here, :] = jnp.broadcast_to(scale[h : h + 1, :], (128, top)).T
        for i, source in enumerate((x_ref, other, far)):

            @pl.when(pick_ref[0] == i)
            def _():
                scaled = source[here, :].astype(F32) * r_ref[here, 0:1]
                normed_ref[here, :] = (scaled * gain_ref[...].astype(F32)).astype(BF16)

    for q in range(8):
        g_ref[slot_ref[q]] = pieces[q][:rows, :]
    for f in range(0, feats, 256):
        turned = normed_ref[:, f : f + 256].T
        for d, out_ref in ((4, p1), (5, m1)) if f < half else ((3, p1), (4, m1)):
            grads = jnp.dot(turned, g_ref[d], preferred_element_type=F32)
            out_ref[f : f + 256, :] = grads.astype(BF16)


def dw_rest_kernel(normed_ref, g_ref, own, p2, p3, p4, m2, m3, m4):
    feats = normed_ref.shape[1]
    half = feats // 2
    uppers = ((0, own), (1, p4), (2, p3), (3, p2), (6, m2), (7, m3))
    lowers = ((0, own), (1, p3), (2, p2), (5, m2), (6, m3), (7, m4))
    for f in range(0, feats, 256):
        turned = normed_ref[:, f : f + 256].T
        for d, out_ref in uppers if f < half else lowers:
            at = f - half if out_ref is m4 else f
            grads = jnp.dot(turned, g_ref[d], preferred_element_type=F32)
            out_ref[at : at + 256, :] = grads.astype(BF16)


def weight_halves(refs):
    held, up1, up2u, up_b, up_c, down1, down2l, down_b, down_c = refs
    half = up2u.shape[0]
    up, lo = slice(0, half), slice(half, 2 * half)
    return (
        (held.at[up], held.at[lo]),
        (up1.at[up], up1.at[lo]),
        (up2u, up_b.at[lo]),
        (up_b.at[up], up_c.at[lo]),
        (up_c.at[up], down_c.at[lo]),
        (down_c.at[up], down_b.at[lo]),
        (down_b.at[up], down2l),
        (down1.at[up], down1.at[lo]),
    )


def y_kernel(model, place_ref, normed_ref, r_ref, g_ref, *rest):
    y_ref = rest[9]
    rows, feats = normed_ref.shape
    half = feats // 2
    inner = None
    for d, (upper, lower) in enumerate(weight_halves(rest[:9])):
        y = jnp.dot(normed_ref[:, :half], upper[...], preferred_element_type=F32)
        y += jnp.dot(normed_ref[:, half:], lower[...], preferred_element_type=F32)
        y_ref[place_ref[d], :rows, :] = y.astype(BF16)
        term = y * g_ref[d].astype(F32)
        inner = term if inner is None else inner + term
    inner = jnp.sum(inner, axis=1, keepdims=True) * jnp.square(r_ref[:, 0:1]) * (1.0 / model)
    line = jnp.broadcast_to(inner, (rows, 128)).T[0:1, :]
    high = line.astype(BF16).astype(F32)
    low = line - high
    row = lax.broadcasted_iota(jnp.int32, (EXTRA, 256), 0)
    tile = jnp.zeros((EXTRA, 256), F32)
    for i, part in enumerate((high[:, :256], high[:, 256:], low[:, :256], low[:, 256:])):
        tile = jnp.where(row == i, jnp.broadcast_to(part, (EXTRA, 256)), tile)
    for b in range(8):
        y_ref[b, rows:, :] = tile.astype(BF16)


def a_kernel(r_ref, gain_ref, g_ref, *rest):
    a_ref, total = rest[9:]
    rows, feats = total.shape
    half = feats // 2
    for d, halves in enumerate(weight_halves(rest[:9])):
        g = g_ref[d]
        for h in range(2):
            here = slice(h * half, (h + 1) * half)
            term = lax.dot_general(
                g, halves[h][...], (((1,), (1,)), ((), ())), preferred_element_type=F32
            )
            if d == 0:
                total[:, here] = term
            else:
                total[:, here] += term
    a_ref[...] = (total[...] * gain_ref[...].astype(F32) * r_ref[:, 0:1]).astype(BF16)


def add_kernel(arrived_ref, own_ref, out_ref):
    out_ref[...] = (arrived_ref[...].astype(F32) + own_ref[...].astype(F32)).astype(BF16)


def last_kernel(plus_ref, minus_ref, plus_u, minus_l, own_ref, out_ref):
    half = plus_u.shape[0]
    for here, x_ref, y_ref in (
        (slice(0, half), plus_u, minus_ref.at[:half]),
        (slice(half, 2 * half), minus_l, plus_ref.at[half:]),
    ):
        total = own_ref[here, :].astype(F32) + x_ref[...].astype(F32) + y_ref[...].astype(F32)
        out_ref[here, :] = total.astype(BF16)


VMEM = pl.BlockSpec(memory_space=pltpu.VMEM)
SMEM = pl.BlockSpec(memory_space=pltpu.SMEM)
ANY = pl.BlockSpec(memory_space=pl.ANY)


def kernel_call(body, name, out_shape, operands, scratch=(), index=1):
    return pl.pallas_call(
        body,
        out_shape=out_shape,
        in_specs=[SMEM] * index + [VMEM] * (len(operands) - index),
        out_specs=[VMEM] * len(out_shape),
        scratch_shapes=list(scratch),
        compiler_params=pltpu.CompilerParams(vmem_limit_bytes=24 * 2**20),
        name=name,
    )(*operands)


def combine(body, name, own, *arrived):
    return pl.pallas_call(
        body,
        out_shape=jax.ShapeDtypeStruct(own.shape, BF16),
        in_specs=[VMEM] * (1 + len(arrived)),
        out_specs=VMEM,
        compiler_params=pltpu.CompilerParams(vmem_limit_bytes=6 * 2**20),
        cost_estimate=pl.CostEstimate(
            flops=own.size, bytes_accessed=6 * own.size, transcendentals=0
        ),
        name=name,
    )(*arrived, own)


def per_device(tokens, norm_gain, held_kv, block_holder, section_layer, cotangent):
    pipe = lax.axis_index("pipe")
    section = lax.axis_index("section")
    pipes = lax.axis_size("pipe")
    tensors = lax.axis_size("tensor")
    micro, tok, feats = tokens.shape[2:]
    rows = micro * tok
    model = feats * tensors
    held = held_kv[0]
    half = feats // 2
    cols = held.shape[1]

    def one(values, index):
        here = jnp.arange(values.shape[0], dtype=jnp.int32) == index
        return jnp.sum(jnp.where(here, values, 0)).reshape(1, 1)

    of_relay = jnp.arange(pipes, dtype=jnp.int32)[:, None] == pipe
    layers = jnp.sum(jnp.where(of_relay, section_layer, 0), axis=0)
    sections = invert(layers)
    every = jnp.arange(layers.shape[0], dtype=jnp.int32)
    near_sources = jnp.where((sections >> 1) == (every >> 1), 1, 0)
    core_sources = jnp.where((sections & 1) == (every & 1), 1, 0)
    near_workers = jnp.where((layers >> 1) == (every >> 1), 1, 0)
    core_workers = jnp.where((layers & 1) == (every & 1), 1, 0)
    source_near, source_core = one(near_sources, section), one(core_sources, section)
    worker_near, worker_core = one(near_workers, section), one(core_workers, section)
    far_source_core = one(core_sources, section ^ 2)
    sibling_worker_near = one(near_workers, section ^ 1)
    tensor = lax.axis_index("tensor")
    even = (1 - (tensor & 1)).reshape(1, 1)
    ids = jnp.arange(tensors, dtype=jnp.int32) ^ (tensor & ~1)
    of_layer = jnp.arange(layers.shape[0], dtype=jnp.int32)[:, None] == section
    holder_row = jnp.sum(jnp.where(of_layer, block_holder, 0), axis=0)
    holders = jnp.sum(
        jnp.where(ids[:, None] == jnp.arange(tensors)[None, :], holder_row[None, :], 0), axis=1
    )
    slots = (holders - pipe) & (pipes - 1)
    places = invert(slots)
    pick = jnp.where(source_near != 0, jnp.where(source_core != 0, 0, 1), 2).reshape(1)
    flags = (
        worker_near,
        worker_core,
        source_near,
        source_core,
        far_source_core,
        sibling_worker_near,
        even,
        slots,
        places,
        pick,
    )

    top = rows // 2
    x_own = tokens.reshape(rows, feats)
    squares = jnp.sum(jnp.square(x_own.astype(F32)), axis=1)
    piece = jnp.concatenate([cotangent.reshape(rows, -1), split_rows(squares)], axis=0)
    held_later = after(held, piece)
    up1, down1 = shift(held_later, "pipe", -1), shift(held_later, "pipe", 1)
    piece_other, x_other = swap(piece, "section", 1), swap(x_own, "section", 1)
    piece_other, flags = lax.optimization_barrier((piece_other, flags))
    (
        worker_near,
        worker_core,
        source_near,
        source_core,
        far_source_core,
        sibling_worker_near,
        even,
        slots,
        places,
        pick,
    ) = flags
    piece_here = choose(source_core, piece, piece_other)
    piece_there = choose(far_source_core, piece, piece_other)
    flip_hi = y_swap(piece_there, 1, 0)
    up2u, down2l = after(up1[:half], piece_here, piece_there), after(down1[half:], piece_here)
    up2u, down2l = shift(up2u, "pipe", -1), shift(down2l, "pipe", 1)
    x_there = choose(far_source_core, x_own, x_other)
    g_own = after(choose(source_near, piece_here, flip_hi), x_there)
    x_far = swap(x_there, "section", 2)
    g_flip = y_swap(g_own, 0, 1)
    up2u, down2l, g_own, g_flip = lax.optimization_barrier((up2u, down2l, g_own, g_flip))

    up_b = shift(jnp.concatenate([up2u, up1[half:]], axis=0), "pipe", -1)
    down_b = shift(jnp.concatenate([down1[:half], down2l], axis=0), "pipe", 1)
    pair = jnp.stack([choose(even, g_own, g_flip), choose(even, g_flip, g_own)])
    g1, g3 = swap(pair, "tensor", 2), swap(pair, "tensor", 6)
    up_b, down_b, g1, g3, pair = lax.optimization_barrier((up_b, down_b, g1, g3, pair))

    up_c, down_c = shift(up_b, "pipe", -1), shift(down_b, "pipe", 1)
    g2a, g2b = swap(g3[0], "tensor", 2), swap(g1[1], "tensor", 6)
    up_c, down_c, g1, g3, g2a, g2b, pair, x_far = lax.optimization_barrier(
        (up_c, down_c, g1, g3, g2a, g2b, pair, x_far)
    )
    weights = (held, up1, up2u, up_b, up_c, down1, down2l, down_b, down_c)

    whole = jax.ShapeDtypeStruct((feats, cols), BF16)
    part = jax.ShapeDtypeStruct((half, cols), BF16)
    normed, r, g, p1, m1 = kernel_call(
        functools.partial(dw_kernel, model),
        "weight_grads",
        (
            jax.ShapeDtypeStruct((rows, feats), BF16),
            jax.ShapeDtypeStruct((rows, 128), F32),
            jax.ShapeDtypeStruct((pipes, rows, cols), BF16),
            whole,
            whole,
        ),
        (slots, pick, x_own, x_other, x_far, norm_gain, pair, g1, g2a, g2b, g3),
        index=2,
    )
    plus, minus = shift(p1, "pipe", 1), shift(m1, "pipe", -1)
    (a,) = kernel_call(
        a_kernel,
        "token_grads",
        (jax.ShapeDtypeStruct((rows, feats), BF16),),
        (r, norm_gain, g, *weights),
        [pltpu.VMEM((rows, feats), F32)],
        index=0,
    )
    (y,) = kernel_call(
        functools.partial(y_kernel, model),
        "keys_values",
        (jax.ShapeDtypeStruct((tensors, rows + EXTRA, cols), BF16),),
        (places, normed, r, after(g, a), *weights),
    )
    own, p2, p3, p4, m2, m3, m4 = kernel_call(
        dw_rest_kernel,
        "more_weight_grads",
        (whole, whole, whole, part, whole, whole, part),
        (after(normed, y, a), g),
        index=0,
    )
    to3, to1 = swap(y[4], "tensor", 2), swap(y[5], "tensor", 6)
    a_far = swap(a, "section", 2)

    def unpack(z):
        lines = z[rows : rows + 4].astype(F32)
        return lines[:2] + lines[2:]

    def total_of(parts):
        total = sum(part.astype(F32) for part in parts)
        return total[:rows].astype(BF16), unpack(total)

    def pack(total):
        return jnp.concatenate([total[0], split_rows(total[1])], axis=0)

    plus, minus = after(plus, y), after(minus, y)
    plus, minus = combine(add_kernel, "add", p2, plus), combine(add_kernel, "add", m2, minus)
    plus, minus, to3, to1 = lax.optimization_barrier((plus, minus, to3, to1))
    plus, minus = shift(plus, "pipe", 1), shift(minus, "pipe", -1)
    send1 = jnp.stack([y[2], pack(total_of([y[3], to1]))])
    send3 = jnp.stack([pack(total_of([y[6], to3])), y[7]])
    got1, got3 = swap(send1, "tensor", 2), swap(send3, "tensor", 6)

    plus, minus = combine(add_kernel, "add", p3, plus), combine(add_kernel, "add", m3, minus)
    plus, minus, got1, got3, a_far = lax.optimization_barrier((plus, minus, got1, got3, a_far))
    plus, minus = shift(plus, "pipe", 1), shift(minus, "pipe", -1)
    parts = [y[:2], got1, got3]
    stays = pack(total_of([choose(even, p[0], p[1]) for p in parts]))
    leaves = pack(total_of([choose(even, p[1], p[0]) for p in parts]))
    flip_lo, flip_hi = y_swap(leaves, 0, 1), y_swap(stays, 1, 0)
    flip_both = y_swap(leaves, 1, 1)

    plus_u = combine(add_kernel, "add", p4, plus[:half])
    minus_l = combine(add_kernel, "add", m4, minus[half:])
    plus_u, minus_l, flip_lo, flip_hi, flip_both = lax.optimization_barrier(
        (plus_u, minus_l, flip_lo, flip_hi, flip_both)
    )
    plus_u, minus_l = shift(plus_u, "pipe", 1), shift(minus_l, "pipe", -1)

    def come_back(here, across):
        other = swap(choose(sibling_worker_near, here, across), "section", 1)
        return choose(worker_core, choose(worker_near, here, across), other)

    packed = come_back(pack(total_of([stays, flip_lo])), pack(total_of([flip_hi, flip_both])))
    keys_values = packed[:rows].reshape(cotangent.shape)
    coef = unpack(packed).reshape(rows, 1)
    a = come_back(a, a_far)
    token_grad = (a.astype(F32) - x_own.astype(F32) * coef).astype(BF16)
    kv_grads = combine(
        last_kernel, "last", own, plus, minus, after(plus_u, token_grad, packed), minus_l
    )[None]
    return (keys_values, token_grad.reshape(tokens.shape), kv_grads)


def solution(mesh):
    placed = (
        P("pipe", "section", None, None, "tensor"),
        P("section", "tensor"),
        P("section", "tensor", "pipe"),
        P(),
        P(),
        P("pipe", "section", None, None, "tensor"),
    )
    return jax.shard_map(
        per_device,
        mesh=mesh,
        in_specs=placed,
        out_specs=(
            P("pipe", "section", None, None, "tensor"),
            P("pipe", "section", None, None, "tensor"),
            P("section", "tensor", "pipe"),
        ),
        check_vma=False,
    )
```
